32 devices in a mesh: groups: 2 (over x), tensor: 8 (over z, y), dp: 2 (over core).
Axes of the slice: x: 2, y: 2, z: 4, core: 2. Of those that a mesh axis runs over, the one named last changes fastest.
Arguments:
- activations: bfloat16 [512, 8192], P(('groups', 'dp'), 'tensor'), parts along dimension 0, may hold values from -640 to 640
- norm_gain: bfloat16 [8192], replicated, may hold values from 0.25 to 1.75
- gate_frozen_weight: bfloat16 [14336, 8192], P(('tensor', 'dp')), may hold values from -0.0625 to 0.0625
- up_frozen_weight: bfloat16 [14336, 8192], P(('tensor', 'dp')), may hold values from -0.0625 to 0.0625
- down_weight: bfloat16 [14336, 8192], P(('tensor', 'dp')), may hold values from -0.046875 to 0.046875
- cotangent: bfloat16 [512, 8192], P(('groups', 'dp'), 'tensor'), parts along dimension 0, may hold values from -6 to 6
- squeeze_master: float32 [256, 8192], P('groups', ('tensor', 'dp')), parts along dimension 0, may hold values from -0.0625 to 0.0625
- squeeze_first: float32 [256, 8192], P('groups', ('tensor', 'dp')), parts along dimension 0, may hold values from -100 to 100
- squeeze_second: float32 [256, 8192], P('groups', ('tensor', 'dp')), parts along dimension 0, may hold values from 100 to 2000
- expand_master: float32 [28672, 128], P(('groups', 'tensor', 'dp')), parts along dimension 0, may hold values from -0.75 to 0.75
- expand_first: float32 [28672, 128], P(('groups', 'tensor', 'dp')), parts along dimension 0, may hold values from -9 to 9
- expand_second: float32 [28672, 128], P(('groups', 'tensor', 'dp')), parts along dimension 0, may hold values from 0.5 to 10
Outputs:
- input_grad: float32 [512, 8192], P(('groups', 'dp'), 'tensor'), parts along dimension 0
- squeeze_master_new: float32 [256, 8192], P('groups', ('tensor', 'dp')), parts along dimension 0
- squeeze_first_new: float32 [256, 8192], P('groups', ('tensor', 'dp')), parts along dimension 0
- squeeze_second_new: float32 [256, 8192], P('groups', ('tensor', 'dp')), parts along dimension 0
- squeeze_adapter: bfloat16 [256, 8192], P('groups', 'tensor'), parts along dimension 0
- expand_master_new: float32 [28672, 128], P(('groups', 'tensor', 'dp')), parts along dimension 0
- expand_first_new: float32 [28672, 128], P(('groups', 'tensor', 'dp')), parts along dimension 0
- expand_second_new: float32 [28672, 128], P(('groups', 'tensor', 'dp')), parts along dimension 0
- expand_adapter: bfloat16 [28672, 128], P(('groups', 'tensor', 'dp')), parts along dimension 0
The draws below stay inside these ranges and needn't reach their ends.
There are 2 independent parts, one for each index of `groups`. The reference program is written for one: setup_inputs(seed, part) draws one part's arguments, and reference() takes and returns one part's arrays. A program takes and returns all parts, laid end to end along the dimension named above; an argument that names none is the same for every part. Nothing has to cross between parts.
All inputs are finite; a program needn't handle non-finite values.
Results may differ from the reference program's by a relative error of at most 0.0055.
Values may be sent and summed in bfloat16 or wider, within the bound.
A program may use at most 128 MiB of HBM per device.

```python
import math
import jax
import jax.numpy as jnp
from jax import lax

D = 8192
FFW = 14336
R = 64
STEP = 20
TOKENS = 256


def draw_activations(key, part):
    first_key, second_key = jax.random.split(jax.random.fold_in(key, 7))
    columns = 10.0 ** (jnp.arange(D, dtype=jnp.float32) / D)
    values = jnp.clip(jax.random.normal(first_key, (TOKENS, D), jnp.float32), -4.0, 4.0)
    row_scales = 10.0 ** jax.random.uniform(second_key, (TOKENS, 1), jnp.float32)
    return (values * row_scales * columns[None, :]).astype(jnp.bfloat16)


def steps_of(key, dims, pieces, low, largest):
    level = 1.0
    for axis_at, blocks in pieces:
        heights = jax.random.uniform(jax.random.fold_in(jax.random.fold_in(key, 6), axis_at), (blocks,), jnp.float32, low / len(pieces), largest / len(pieces))
        level = level * jnp.repeat(jnp.exp(heights), dims[axis_at] // blocks).reshape((-1,) + (1,) * (len(dims) - 1 - axis_at))
    return level


def scatter_about(own_key, extent, spread, limit, cuts=(), kind=jnp.bfloat16):
    array = spread * jax.random.normal(own_key, extent, jnp.float32)
    if cuts:
        array = array * steps_of(own_key, extent, cuts, -0.22, 0.18)
    return jnp.clip(array, -limit, limit).astype(kind)


def setup_inputs(seed: int = 0, part: int = 0) -> dict:
    splits = jax.random.split(jax.random.key(seed), 13)
    part_keys = jax.random.split(jax.random.fold_in(splits[12], part), 13)
    return {
        "activations": draw_activations(jax.random.fold_in(jax.random.fold_in(splits[12], part), 71), part),
        "norm_gain": jnp.clip(1.0 + 0.15 * jax.random.normal(splits[1], (D,), jnp.float32), 0.25, 1.75).astype(jnp.bfloat16),
        "gate_frozen_weight": scatter_about(splits[2], (FFW, D), D ** -0.5, 0.0625, ((0, 16),)),
        "up_frozen_weight": scatter_about(splits[3], (FFW, D), D ** -0.5, 0.0625, ((0, 16),)),
        "down_weight": scatter_about(splits[4], (FFW, D), FFW ** -0.5, 0.046875, ((0, 16),)),
        "cotangent": scatter_about(part_keys[5], (TOKENS, D), 1.0, 6.0, ((0, 2), (1, 8))),
        "squeeze_master": scatter_about(part_keys[6], (2 * R, D), D ** -0.5, 0.0625, ((1, 16),), jnp.float32),
        "squeeze_first": scatter_about(part_keys[7], (2 * R, D), 20.0, 100.0, ((1, 16),), jnp.float32),
        "squeeze_second": jnp.clip(jnp.exp(math.log(2000.0) - 2.9957323 * jax.random.uniform(part_keys[8], (2 * R, D), jnp.float32) ** steps_of(part_keys[8], (2 * R, D), ((1, 16),), -0.2, 0.2)), 100.0, 2000.0),
        "expand_master": scatter_about(part_keys[9], (FFW, 2 * R), R ** -0.5, 0.75, ((0, 16),), jnp.float32),
        "expand_first": scatter_about(part_keys[10], (FFW, 2 * R), 1.5, 9.0, ((0, 16),), jnp.float32),
        "expand_second": jnp.clip(jnp.exp(math.log(10.0) - 2.9957323 * jax.random.uniform(part_keys[11], (FFW, 2 * R), jnp.float32) ** steps_of(part_keys[11], (FFW, 2 * R), ((0, 16),), -0.2, 0.2)), 0.5, 10.0),
    }


adapter_output_scale = 0.25
norm_epsilon = 1e-05
learning_rate = 0.001
decay_rate = 0.1
beta_first = 0.9
beta_second = 0.95
adam_epsilon = 1e-08

def adamw_update(master, first, second, grads):
    first_new = beta_first * first + (1.0 - beta_first) * grads
    second_new = beta_second * second + (1.0 - beta_second) * grads * grads
    first_hat = first_new / (1.0 - beta_first ** STEP)
    second_hat = second_new / (1.0 - beta_second ** STEP)
    master_new = master - learning_rate * (first_hat / (jnp.sqrt(second_hat) + adam_epsilon) + decay_rate * master)
    return (master_new, first_new, second_new)

def reference(activations, norm_gain, gate_frozen_weight, up_frozen_weight, down_weight, cotangent, squeeze_master, squeeze_first, squeeze_second, expand_master, expand_first, expand_second):
    input_float = activations.astype(jnp.float32)
    gain_float = norm_gain.astype(jnp.float32)
    scale_rows = lax.rsqrt(lax.optimization_barrier(jnp.mean(input_float * input_float, axis=1)) + norm_epsilon)
    normalized_rows = (input_float * scale_rows[:, None] * gain_float).astype(jnp.bfloat16)
    squeeze_current = squeeze_master.astype(jnp.bfloat16)
    expand_factor_now = expand_master.astype(jnp.bfloat16)
    adapter_inner_rank = expand_factor_now.shape[1] // 2
    reduced_features = jnp.dot(normalized_rows, squeeze_current.T, preferred_element_type=jnp.float32).astype(jnp.bfloat16)
    gate_preactivation = jnp.dot(normalized_rows, gate_frozen_weight.T, preferred_element_type=jnp.float32) + adapter_output_scale * jnp.dot(reduced_features[:, :adapter_inner_rank], expand_factor_now[:, :adapter_inner_rank].T, preferred_element_type=jnp.float32)
    up_preactivation = jnp.dot(normalized_rows, up_frozen_weight.T, preferred_element_type=jnp.float32) + adapter_output_scale * jnp.dot(reduced_features[:, adapter_inner_rank:], expand_factor_now[:, adapter_inner_rank:].T, preferred_element_type=jnp.float32)
    hidden_grad = jnp.dot(cotangent, down_weight.T, preferred_element_type=jnp.float32)
    sigmoid_gate = jax.nn.sigmoid(gate_preactivation)
    gate_branch_gradient = (hidden_grad * up_preactivation * sigmoid_gate * (1.0 + gate_preactivation * (1.0 - sigmoid_gate))).astype(jnp.bfloat16)
    up_branch_gradient = (hidden_grad * gate_preactivation * sigmoid_gate).astype(jnp.bfloat16)
    reduced_gradient = adapter_output_scale * jnp.concatenate([jnp.dot(gate_branch_gradient, expand_factor_now[:, :adapter_inner_rank], preferred_element_type=jnp.float32), jnp.dot(up_branch_gradient, expand_factor_now[:, adapter_inner_rank:], preferred_element_type=jnp.float32)], axis=1)
    reduced_gradient = reduced_gradient.astype(jnp.bfloat16)
    normed_grad = jnp.dot(gate_branch_gradient, gate_frozen_weight, preferred_element_type=jnp.float32) + jnp.dot(up_branch_gradient, up_frozen_weight, preferred_element_type=jnp.float32) + jnp.dot(reduced_gradient, squeeze_current, preferred_element_type=jnp.float32)
    row_dot = lax.optimization_barrier(jnp.sum(normed_grad * input_float * gain_float, axis=1))
    input_grad = scale_rows[:, None] * gain_float * normed_grad - input_float * (scale_rows ** 3)[:, None] * row_dot[:, None] / D
    squeeze_grad = jnp.dot(reduced_gradient.T, normalized_rows, preferred_element_type=jnp.float32)
    expand_factor_gradient = adapter_output_scale * jnp.concatenate([jnp.dot(gate_branch_gradient.T, reduced_features[:, :adapter_inner_rank], preferred_element_type=jnp.float32), jnp.dot(up_branch_gradient.T, reduced_features[:, adapter_inner_rank:], preferred_element_type=jnp.float32)], axis=1)
    squeeze_new, squeeze_first_new, squeeze_second_new = adamw_update(squeeze_master, squeeze_first, squeeze_second, squeeze_grad)
    expand_new, expand_first_new, expand_second_new = adamw_update(expand_master, expand_first, expand_second, expand_factor_gradient)
    return (input_grad, squeeze_new, squeeze_first_new, squeeze_second_new, squeeze_new.astype(jnp.bfloat16), expand_new, expand_first_new, expand_second_new, expand_new.astype(jnp.bfloat16))
```

```python
import functools

import jax
import jax.numpy as jnp
from jax import lax
from jax.experimental import pallas as pl
from jax.experimental.pallas import tpu as pltpu
from jax.sharding import PartitionSpec as P

STEP = 20
MESH = pl.DeviceIdType.MESH
F32 = jnp.float32
BF16 = jnp.bfloat16

adapter_output_scale = 0.25
norm_epsilon = 1e-05
learning_rate = 0.001
decay_rate = 0.1
beta_first = 0.9
beta_second = 0.95
adam_epsilon = 1e-08


def dot_t(left, right):
    return lax.dot_general(left, right, (((1,), (1,)), ((), ())), preferred_element_type=F32)


def dot_rows(left, right):
    return lax.dot_general(left, right, (((0,), (0,)), ((), ())), preferred_element_type=F32)


def dot_n(left, right):
    return jnp.dot(left, right, preferred_element_type=F32)


def adamw_update(master, first, second, grads):
    first_new = beta_first * first + (1.0 - beta_first) * grads
    second_new = beta_second * second + (1.0 - beta_second) * grads * grads
    first_hat = first_new / (1.0 - beta_first**STEP)
    second_hat = second_new / (1.0 - beta_second**STEP)
    master_new = master - learning_rate * (
        first_hat / (jnp.sqrt(second_hat) + adam_epsilon) + decay_rate * master
    )
    return (master_new, first_new, second_new)


def layer_kernel(
    T,
    act, cot, gain, wg, wu, wd, sqm, sqf, sqs, exm, exf, exs,
    out_grad, o_sqm, o_sqf, o_sqs, o_sqa, o_exm, o_exf, o_exs, o_exa,
    G, WG, WU, HID, AG, AU, GG, UG, EX, EB, SQ, SQV, SC, LOW, LGP, LGR, LGF,
    YS4, YR4, ZS4, ZR4, PO, CSS, CSR, YS, YR, ZS, ZR, SQA, EA,
    sG, rG, wsem, lsem, osem, sSib, rSib, sY4, rY4, sZ4, rZ4,
    sCS, rCS, sYR, rYR, sZR, rZR,
):
    Z = T // 2
    n = 2 * Z - 1
    S = act.shape[1]
    H = wg.shape[0]
    rows = act.shape[0]
    width = S * T
    Q = sqm.shape[1]
    me = lax.axis_index("tensor")
    c = lax.axis_index("dp")
    z = me // 2
    y = me % 2
    sib = {"tensor": me, "dp": 1 - c}
    yp = {"tensor": z * 2 + (1 - y), "dp": c}

    def zdev(zz):
        return {"tensor": zz * 2 + y, "dp": c}

    def rc(src, dst, ss, rs, dev):
        return pltpu.make_async_remote_copy(
            src_ref=src, dst_ref=dst, send_sem=ss, recv_sem=rs,
            device_id=dev, device_id_type=MESH,
        )

    def item(i):
        d = (i + 1) // 2
        zz = z + (2 * (i % 2) - 1) * d
        return zz, jnp.logical_and(zz >= 0, zz < Z)

    def wcopy(m, t):
        src = (wg, wu, wd)[m]
        dst = (WG, WU, WU)[m]
        return pltpu.make_async_copy(
            src.at[:, pl.ds(pl.multiple_of(t * S, S), S)], dst.at[t], wsem.at[m, t]
        )

    ex_in = (exm, exf, exs)
    sq_in = (sqm, sqf, sqs)
    ex_out = (o_exm, o_exf, o_exs)
    sq_out = (o_sqm, o_sqf, o_sqs)
    sq_load = [pltpu.make_async_copy(sq_in[k], SQV.at[k], lsem.at[k]) for k in range(3)]
    ex_load = [pltpu.make_async_copy(ex_in[k], EX.at[k], lsem.at[3 + k]) for k in range(3)]
    for cp in sq_load + ex_load:
        cp.start()

    barrier = pltpu.get_barrier_semaphore()
    pl.semaphore_signal(barrier, inc=1, device_id=sib, device_id_type=MESH)
    pl.semaphore_signal(barrier, inc=1, device_id=yp, device_id_type=MESH)

    @pl.loop(1, Z)
    def _(j):
        pl.semaphore_signal(barrier, inc=1, device_id=zdev((z + j) % Z), device_id_type=MESH)

    def load_weights(m):
        @pl.loop(0, n)
        def _(i):
            zz, ok = item(i)

            @pl.when(ok)
            def _():
                wcopy(m, zz * 2 + y).start()
                wcopy(m, zz * 2 + 1 - y).start()

    load_weights(2)
    load_weights(0)

    G[0, me, c] = cot[...]
    xf = act[...].astype(F32)
    YS4[0] = jnp.broadcast_to(jnp.sum(xf * xf, axis=1, keepdims=True), (rows, 128))
    pl.semaphore_wait(barrier, Z + 1)

    def ar_y(k):
        return rc(YS4.at[k], YR4.at[k], sY4.at[k], rY4.at[k], yp)

    def ar_z(k, j):
        return rc(ZS4.at[k], ZR4.at[k, z], sZ4.at[k, j], rZ4.at[k, z], zdev((z + j) % Z))

    def ar_mid(k):
        ar_y(k).wait_recv()
        ZS4[k] = YS4[k] + YR4[k]

        @pl.loop(1, Z)
        def _(j):
            ar_z(k, j).start()

    def ar_end(k):
        YR4[k] = ZS4[k]

        @pl.loop(1, Z)
        def _(j):
            o = (z + j) % Z
            rc(ZS4.at[k], ZR4.at[k, o], sZ4.at[k, j], rZ4.at[k, o], zdev(o)).wait_recv()
            YR4[k] = YR4[k] + ZR4[k, o]

        return YR4[k]

    def ar_drain(k):
        ar_y(k).wait_send()

        @pl.loop(1, Z)
        def _(j):
            ar_z(k, j).wait_send()

    def slot_send(a, t, k, dev):
        return rc(G.at[a, t, c], G.at[a, t, c], sG.at[a, t, k], rG.at[a, t, c], dev)

    def slot_recv(a, t, cc):
        rc(G.at[a, t, cc], G.at[a, t, cc], sG.at[a, t, 0], rG.at[a, t, cc], sib).wait_recv()

    def forward(a, zz, op):
        t = zz * 2 + y

        @pl.when(jnp.logical_and(zz <= z, z + 1 < Z))
        def _():
            op(slot_send(a, t, 0, zdev(z + 1)))

        @pl.when(jnp.logical_and(zz >= z, z > 0))
        def _():
            op(slot_send(a, t, 1, zdev(z - 1)))

        op(slot_send(a, t, 2, yp))
        op(slot_send(a, t, 3, sib))

    def begin(cp):
        cp.start()

    ar_y(0).start()
    forward(0, z, begin)
    sq_load[0].wait()
    SQ[c] = SQV[0].astype(BF16)
    sq_send = rc(SQ.at[c], SQ.at[c], sSib.at[0], rSib.at[0], sib)
    sq_send.start()
    HID[...] = jnp.zeros_like(HID)
    AG[...] = jnp.zeros_like(AG)
    AU[...] = jnp.zeros_like(AU)
    ar_mid(0)
    SC[...] = lax.rsqrt(ar_end(0) / width + norm_epsilon)
    G[1, me, c] = (act[...].astype(F32) * SC[:, :1] * gain[...]).astype(BF16)
    forward(1, z, begin)
    rc(SQ.at[1 - c], SQ.at[1 - c], sSib.at[0], rSib.at[0], sib).wait_recv()
    own = G[1, me, c]
    YS4[1] = dot_t(own[:, :Q], SQ[0]) + dot_t(own[:, Q:], SQ[1])
    ar_y(1).start()

    low_send = rc(LOW.at[c], LOW.at[c], sSib.at[1], rSib.at[1], sib)

    @pl.loop(0, 2 * n + 3)
    def _(g):
        @pl.when(g < 2 * n)
        def _():
            a, i = g // n, g % n
            zz, ok = item(i)

            @pl.when(jnp.logical_and(ok, i > 0))
            def _():
                slot_recv(a, zz * 2 + y, c)
                forward(a, zz, begin)

        @pl.when(jnp.logical_and(g >= 2, g < 2 * n + 2))
        def _():
            a, i = (g - 2) // n, (g - 2) % n
            zz, ok = item(i)

            @pl.when(ok)
            def _():
                t = zz * 2 + 1 - y
                slot_recv(a, t, c)
                slot_send(a, t, 3, sib).start()

        @pl.when(g >= 3)
        def _():
            a, i = (g - 3) // n, (g - 3) % n
            zz, ok = item(i)

            @pl.when(ok)
            def _():
                @pl.loop(0, 2)
                def _(r):
                    t = zz * 2 + (y + r) % 2
                    slot_recv(a, t, 1 - c)

                    @pl.when(a == 0)
                    def _():
                        wcopy(2, t).wait()
                        block = G[0, t].reshape(2 * rows, S)
                        HID[...] += dot_t(block, WU[t])
                        wcopy(1, t).start()

                    @pl.when(a == 1)
                    def _():
                        block = G[1, t].reshape(2 * rows, S)
                        wcopy(0, t).wait()
                        AG[...] += dot_t(block, WG[t])
                        wcopy(1, t).wait()
                        AU[...] += dot_t(block, WU[t])

        @pl.when(g == 2)
        def _():
            ar_mid(1)

        @pl.when(g == n)
        def _():
            LOW[c] = ar_end(1).astype(BF16)
            low_send.start()

    rc(LOW.at[1 - c], LOW.at[1 - c], sSib.at[1], rSib.at[1], sib).wait_recv()
    for cp in ex_load:
        cp.wait()
    EB[...] = EX[0].astype(BF16)
    rank = EB.shape[1] // 2
    chunk = 64
    per = rows // chunk

    @pl.loop(0, 2 * per)
    def _(q):
        h, r = q // per, q % per
        inner = pl.ds(pl.multiple_of(r * chunk, chunk), chunk)
        sl = pl.ds(pl.multiple_of(q * chunk, chunk), chunk)
        low = LOW[h, inner]
        left = lax.broadcasted_iota(jnp.int32, low.shape, 1) < rank
        zero = jnp.zeros_like(low)
        b = EB[...]
        gate = AG[sl] + adapter_output_scale * dot_t(jnp.where(left, low, zero), b)
        up = AU[sl] + adapter_output_scale * dot_t(jnp.where(left, zero, low), b)
        hid = HID[sl]
        s = jax.nn.sigmoid(gate)
        gg = (hid * up * s * (1.0 + gate * (1.0 - s))).astype(BF16)
        ug = (hid * gate * s).astype(BF16)
        GG[sl] = gg
        UG[sl] = ug
        LGP[h, 0, inner] = adapter_output_scale * jnp.where(left, dot_n(gg, b), dot_n(ug, b))
        dots = jnp.sum(gg.astype(F32) * gate + ug.astype(F32) * up, axis=1, keepdims=True)
        LGP[h, 1, inner] = jnp.broadcast_to(dots, (chunk, 128))

    lg_send = rc(LGP.at[1 - c], LGR, sSib.at[2], rSib.at[2], sib)
    lg_send.start()
    lgf_send = rc(LGF.at[c], LGF.at[c], sSib.at[3], rSib.at[3], sib)

    def cs_copy(t):
        return rc(CSS.at[t], CSR.at[t], sCS.at[t], rCS.at[t], sib)

    def yr_copy(zz):
        return rc(YS.at[zz], YR.at[zz], sYR.at[zz], rYR.at[zz], yp)

    def right_copy(zz):
        return rc(ZS.at[zz], ZR.at[0, zz], sZR.at[zz], rZR.at[0, zz], zdev(z + 1))

    def left_copy(zz):
        return rc(ZS.at[zz], ZR.at[1, zz], sZR.at[zz], rZR.at[1, zz], zdev(z - 1))

    def chain_recv(way, zz):
        rc(ZS.at[zz], ZR.at[way, zz], sZR.at[zz], rZR.at[way, zz], sib).wait_recv()

    def chain(zz):
        t = zz * 2 + y
        yr_copy(zz).wait_recv()
        PO[t] = PO[t] + YR[zz].astype(F32)

        @pl.when(jnp.logical_and(zz >= z, z > 0))
        def _():
            chain_recv(0, zz)
            PO[t] = PO[t] + ZR[0, zz].astype(F32)

        @pl.when(jnp.logical_and(zz <= z, z + 1 < Z))
        def _():
            chain_recv(1, zz)
            PO[t] = PO[t] + ZR[1, zz].astype(F32)

        @pl.when(zz > z)
        def _():
            ZS[zz] = PO[t].astype(BF16)
            right_copy(zz).start()

        @pl.when(zz < z)
        def _():
            ZS[zz] = PO[t].astype(BF16)
            left_copy(zz).start()

    @pl.loop(0, 2 * n + 2)
    def _(g):
        @pl.when(g < 2 * n)
        def _():
            p, i = g // n, n - 1 - g % n
            zz, ok = item(i)

            @pl.when(ok)
            def _():
                t = zz * 2 + (1 - y + p) % 2
                part = dot_n(GG[...], WG[t]) + dot_n(UG[...], WU[t])
                part = part.reshape(2, rows, S)

                @pl.when(c == 0)
                def _():
                    PO[t] = part[0]
                    CSS[t] = part[1].astype(BF16)

                @pl.when(c == 1)
                def _():
                    PO[t] = part[1]
                    CSS[t] = part[0].astype(BF16)

                cs_copy(t).start()

        @pl.when(jnp.logical_and(g >= 1, g < 2 * n + 1))
        def _():
            p, i = (g - 1) // n, n - 1 - (g - 1) % n
            zz, ok = item(i)

            @pl.when(ok)
            def _():
                t = zz * 2 + (1 - y + p) % 2
                cs_copy(t).wait_recv()
                PO[t] = PO[t] + CSR[t].astype(F32)

                @pl.when(p == 0)
                def _():
                    YS[zz] = PO[t].astype(BF16)
                    yr_copy(zz).start()

        @pl.when(g >= n + 2)
        def _():
            i = n - 1 - (g - n - 2)
            zz, ok = item(i)

            @pl.when(jnp.logical_and(ok, i > 0))
            def _():
                chain(zz)

        @pl.when(g == 2)
        def _():
            lg_send.wait_recv()
            YS4[2] = LGP[c, 0] + LGR[0]
            YS4[3] = LGP[c, 1] + LGR[1]
            ar_y(2).start()
            ar_y(3).start()

        @pl.when(g == n - 1)
        def _():
            ar_mid(2)
            ar_mid(3)

        @pl.when(g == n + 2)
        def _():
            LGF[c] = ar_end(2).astype(BF16)
            lgf_send.start()

    low = LOW[...].reshape(2 * rows, 2 * rank)
    left = lax.broadcasted_iota(jnp.int32, low.shape, 1) < rank
    zero = jnp.zeros_like(low)
    grads = adapter_output_scale * (
        dot_rows(GG[...], jnp.where(left, low, zero)) + dot_rows(UG[...], jnp.where(left, zero, low))
    )
    new = adamw_update(EX[0], EX[1], EX[2], grads)
    for k in range(3):
        EX[k] = new[k]
    EA[...] = new[0].astype(BF16)
    stores = [pltpu.make_async_copy(EX.at[k], ex_out[k], osem.at[k]) for k in range(3)]
    stores.append(pltpu.make_async_copy(EA, o_exa, osem.at[3]))
    for cp in stores:
        cp.start()
    for cp in sq_load[1:]:
        cp.wait()
    rc(LGF.at[1 - c], LGF.at[1 - c], sSib.at[3], rSib.at[3], sib).wait_recv()
    cols = pl.ds(pl.multiple_of(c * Q, Q), Q)
    sgrads = dot_rows(LGF[0], G[1, me, 0, :, cols]) + dot_rows(LGF[1], G[1, me, 1, :, cols])
    snew = adamw_update(SQV[0], SQV[1], SQV[2], sgrads)
    for k in range(3):
        SQV[k] = snew[k]
    SQA[c] = snew[0].astype(BF16)
    sqa_send = rc(SQA.at[c], SQA.at[c], sSib.at[4], rSib.at[4], sib)
    sqa_send.start()
    more = [pltpu.make_async_copy(SQV.at[k], sq_out[k], osem.at[4 + k]) for k in range(3)]
    for cp in more:
        cp.start()
    row_dot = ar_end(3)[:, :1]
    chain(z)
    lo = LGF[c]
    scale = SC[:, :1]
    for k in range(2):
        fs = slice(k * Q, (k + 1) * Q)
        ng = PO[me, :, fs] + dot_n(lo, SQ[k])
        out_grad[:, fs] = scale * gain[:, fs] * ng - act[:, fs].astype(F32) * (
            scale * scale * row_dot / width
        )
    rc(SQA.at[1 - c], SQA.at[1 - c], sSib.at[4], rSib.at[4], sib).wait_recv()
    for k in range(2):
        o_sqa[:, k * Q:(k + 1) * Q] = SQA[k]

    for cp in stores + more:
        cp.wait()
    for cp in (sq_send, low_send, lg_send, lgf_send, sqa_send):
        cp.wait_send()
    for k in range(4):
        ar_drain(k)

    def sent(cp):
        cp.wait_send()

    @pl.loop(0, Z)
    def _(zz):
        for a in range(2):
            forward(a, zz, sent)
            slot_send(a, zz * 2 + 1 - y, 3, sib).wait_send()
        cs_copy(zz * 2).wait_send()
        cs_copy(zz * 2 + 1).wait_send()
        yr_copy(zz).wait_send()

        @pl.when(zz > z)
        def _():
            right_copy(zz).wait_send()

        @pl.when(zz < z)
        def _():
            left_copy(zz).wait_send()


def on_device(
    T, activations, norm_gain, gate, up, down, cotangent,
    sqm, sqf, sqs, exm, exf, exs,
):
    rows, S = activations.shape
    H = gate.shape[0]
    Z = T // 2
    ranks, Q = sqm.shape
    index = lax.axis_index("tensor")
    gain = lax.dynamic_slice_in_dim(norm_gain, index * S, S).astype(F32)[None, :]
    vmem = pl.BlockSpec(memory_space=pltpu.VMEM)
    hbm = pl.BlockSpec(memory_space=pl.ANY)
    DMA = pltpu.SemaphoreType.DMA
    V = pltpu.VMEM
    shape = jax.ShapeDtypeStruct
    return pl.pallas_call(
        functools.partial(layer_kernel, T),
        out_shape=(
            shape((rows, S), F32), shape(sqm.shape, F32), shape(sqm.shape, F32),
            shape(sqm.shape, F32), shape((ranks, 2 * Q), BF16), shape(exm.shape, F32),
            shape(exm.shape, F32), shape(exm.shape, F32), shape(exm.shape, BF16),
        ),
        in_specs=[vmem, vmem, vmem] + [hbm] * 9,
        out_specs=(vmem, hbm, hbm, hbm, vmem, hbm, hbm, hbm, hbm),
        scratch_shapes=[
            V((2, T, 2, rows, S), BF16),
            V((T, H, S), BF16), V((T, H, S), BF16),
            V((2 * rows, H), F32), V((2 * rows, H), F32), V((2 * rows, H), F32),
            V((2 * rows, H), BF16), V((2 * rows, H), BF16),
            V((3,) + exm.shape, F32), V(exm.shape, BF16),
            V((2, ranks, Q), BF16), V((3, ranks, Q), F32),
            V((rows, 128), F32),
            V((2, rows, ranks), BF16), V((2, 2, rows, 128), F32), V((2, rows, 128), F32),
            V((2, rows, ranks), BF16),
            V((4, rows, 128), F32), V((4, rows, 128), F32), V((4, rows, 128), F32),
            V((4, Z, rows, 128), F32),
            V((T, rows, S), F32), V((T, rows, S), BF16), V((T, rows, S), BF16),
            V((Z, rows, S), BF16), V((Z, rows, S), BF16), V((Z, rows, S), BF16),
            V((2, Z, rows, S), BF16),
            V((2, ranks, Q), BF16), V(exm.shape, BF16),
            DMA((2, T, 4)), DMA((2, T, 2)), DMA((3, T)), DMA((6,)), DMA((8,)),
            DMA((5,)), DMA((5,)), DMA((4,)), DMA((4,)), DMA((4, Z)), DMA((4, Z)),
            DMA((T,)), DMA((T,)), DMA((Z,)), DMA((Z,)), DMA((Z,)), DMA((2, Z)),
        ],
        compiler_params=pltpu.CompilerParams(
            collective_id=0, has_side_effects=True, vmem_limit_bytes=63 * 2**20
        ),
    )(activations, cotangent, gain, gate, up, down, sqm, sqf, sqs, exm, exf, exs)


def solution(mesh):
    rows = P(("groups", "dp"), "tensor")
    hidden = P(("tensor", "dp"), None)
    sq = P("groups", ("tensor", "dp"))
    ex = P(("groups", "tensor", "dp"), None)
    return jax.shard_map(
        functools.partial(on_device, mesh.shape["tensor"]),
        mesh=mesh,
        in_specs=(rows, P(), hidden, hidden, hidden, rows, sq, sq, sq, ex, ex, ex),
        out_specs=(rows, sq, sq, sq, P("groups", "tensor"), ex, ex, ex, ex),
        check_vma=False,
    )
```
